32 devices in a mesh: dp: 8 (over y, x, core), mp: 4 (over z).
Axes of the slice: x: 2, y: 2, z: 4, core: 2. Of those that a mesh axis runs over, the one named last changes fastest.
Arguments:
- activations: bfloat16 [1024, 8192], P('dp'), may hold values from -16 to 16
- out_grads: bfloat16 [1024, 16384], P('dp', 'mp'), may hold values from -1 to 1
- weight: float32 [8192, 16384], P('dp', 'mp'), may hold values from -16 to 16
- row_moment: float32 [8192], P('dp'), may hold values from 0.25 to 2
- col_moment: float32 [16384], P('mp'), may hold values from 0.25 to 2
Outputs:
- update: float32 [8192, 16384], P('dp', 'mp')
- new_rows: float32 [8192], P('dp')
- new_cols: float32 [16384], P('mp')
The draws below stay inside these ranges and needn't reach their ends.
All inputs are finite; a program needn't handle non-finite values.
Results may differ from the reference program's by a relative error of at most 0.0003.
Values may be sent and summed in bfloat16 or wider, within the bound.
A program may use at most 128 MiB of HBM per device.

```python
import math
import jax
import jax.numpy as jnp
from jax import lax

D = 8192
FF = 16384
TOKENS = 1024


def column_scales(key, count):
    spread = jnp.exp(jax.random.uniform(key, (count,), jnp.float32, math.log(0.5), math.log(2.0)))
    ramp = 0.5 + jnp.arange(count, dtype=jnp.float32) / count
    return ramp * spread


def shared_parts(key):
    key = jax.random.fold_in(key, 5)
    key_token, key_group, key_row, key_col = jax.random.split(key, 4)
    strength = jnp.clip(jax.random.normal(key_token, (TOKENS, 1), jnp.float32), -4.0, 4.0)
    group = jax.random.randint(key_group, (TOKENS, 1), 0, 2).astype(jnp.float32)
    row_dir = jnp.clip(jax.random.normal(key_row, (D,), jnp.float32), -4.0, 4.0)
    col_dir = jnp.clip(jax.random.normal(key_col, (FF,), jnp.float32), -4.0, 4.0)
    return (strength, group, row_dir, col_dir)


def feature_gain(key, count, group):
    side = jax.random.randint(key, (count,), 0, 2).astype(jnp.float32)
    first = 1.0 - side
    return (1.0 - group) * (1.0 + 2.0 * first[None, :]) + group * (1.0 + 0.5 * side[None, :])


def draw_activations(key, part):
    strength, group, row_dir, col_dir = shared_parts(key)
    coupling = math.sqrt(0.4 / math.sqrt(TOKENS))
    key = jax.random.fold_in(key, 11)
    key_scale = jax.random.fold_in(key, 0)
    key_base = jax.random.fold_in(key, 1)
    key_side = jax.random.fold_in(key, 3)
    column_scale = column_scales(key_scale, D)
    gain = feature_gain(key_side, D, group)
    coupled = coupling * strength * row_dir[None, :]
    base = jnp.clip(jax.random.normal(key_base, (TOKENS, D), jnp.float32), -6.0, 6.0)
    values = (base + coupled) * gain * column_scale[None, :]
    return jnp.clip(values, -16.0, 16.0).astype(jnp.bfloat16)


def draw_out_grads(key, part):
    strength, group, row_dir, col_dir = shared_parts(key)
    coupling = math.sqrt(0.4 / math.sqrt(TOKENS))
    key = jax.random.fold_in(key, 23)
    key_scale = jax.random.fold_in(key, 0)
    key_base = jax.random.fold_in(key, 1)
    key_side = jax.random.fold_in(key, 4)
    column_scale = column_scales(key_scale, FF) / math.sqrt(TOKENS)
    gain = feature_gain(key_side, FF, group)
    coupled = coupling * strength * col_dir[None, :]
    base = jnp.clip(jax.random.normal(key_base, (TOKENS, FF), jnp.float32), -6.0, 6.0)
    values = (base + coupled) * gain * column_scale[None, :]
    return jnp.clip(values, -1.0, 1.0).astype(jnp.bfloat16)


def draw_weight(key, part):
    strength, group, row_dir, col_dir = shared_parts(key)
    key = jax.random.fold_in(key, 37)
    key_rows, key_base = jax.random.split(key, 2)
    row_scale = column_scales(key_rows, D)
    column_ramp = 0.5 + jnp.arange(FF, dtype=jnp.float32) / FF
    aligned = 0.5 * row_dir[:, None] * col_dir[None, :]
    base = jnp.clip(jax.random.normal(key_base, (D, FF), jnp.float32), -6.0, 6.0)
    values = (base + aligned) * row_scale[:, None] * column_ramp[None, :]
    return jnp.clip(values, -16.0, 16.0)


def block_levels(stream_key, shape, shards, least, top_value):
    def one(position, parts):
        heights = jax.random.uniform(jax.random.fold_in(jax.random.fold_in(stream_key, 6), position), (parts,), jnp.float32, least / len(shards), top_value / len(shards))
        return jnp.repeat(jnp.exp(heights), shape[position] // parts).reshape((-1,) + (1,) * (len(shape) - position - 1))

    level = one(*shards[0])
    for cut in shards[1:]:
        level = level * one(*cut)
    return level


def setup_inputs(seed: int = 0) -> dict:
    key_of = jax.random.split(jax.random.key(seed), 6)
    return {
        "activations": draw_activations(jax.random.fold_in(key_of[5], 71), 0),
        "out_grads": draw_out_grads(jax.random.fold_in(key_of[5], 71), 0),
        "weight": draw_weight(jax.random.fold_in(key_of[5], 71), 0),
        "row_moment": jnp.clip(jnp.exp(math.log(2.0) - 2.0794415 * jax.random.uniform(key_of[3], (D,), jnp.float32) ** block_levels(key_of[3], (D,), ((0, 8),), -0.2, 0.2)), 0.25, 2.0),
        "col_moment": jnp.clip(jnp.exp(math.log(2.0) - 2.0794415 * jax.random.uniform(key_of[4], (FF,), jnp.float32) ** block_levels(key_of[4], (FF,), ((0, 4),), -0.2, 0.2)), 0.25, 2.0),
    }


BETA_TWO = 0.8
CLIP_LEVEL = 0.25
WEIGHT_DECAY = 0.1
EPSILON = 1e-06

def reference(activations, out_grads, weight, row_moment, col_moment):
    weight_grad = jnp.dot(activations.T, out_grads, preferred_element_type=jnp.float32)
    squares = weight_grad * weight_grad
    new_rows = BETA_TWO * row_moment + (1.0 - BETA_TWO) * (lax.optimization_barrier(jnp.sum(squares, axis=1)) / FF)
    new_cols = BETA_TWO * col_moment + (1.0 - BETA_TWO) * (lax.optimization_barrier(jnp.sum(squares, axis=0)) / D)
    scaled = weight_grad / jnp.sqrt(new_rows[:, None] * new_cols[None, :])
    mean_square = jnp.sum(scaled * scaled) / (D * FF)
    factor = 1.0 / jnp.maximum(1.0, jnp.sqrt(mean_square) / CLIP_LEVEL)
    direction = factor * scaled + WEIGHT_DECAY * weight
    trust_ratio = jnp.sqrt(jnp.sum(weight * weight) / (jnp.sum(direction * direction) + EPSILON))
    return (trust_ratio * direction, new_rows, new_cols)
```

```python
import functools
import math

import jax
import jax.numpy as jnp
from jax import lax
from jax.experimental import pallas as pl
from jax.experimental.pallas import tpu as pltpu
from jax.sharding import PartitionSpec as P

D = 8192
FF = 16384

BETA_TWO = 0.8
CLIP_LEVEL = 0.25
WEIGHT_DECAY = 0.1
EPSILON = 1e-06

MESH = pl.DeviceIdType.MESH
F32 = jnp.float32
BLOCKS = 4
SHARE = 2
LANES = 128


def grid_of(chips):
    wide = max(k for k in range(1, math.isqrt(chips) + 1) if chips % k == 0)
    return chips // wide, wide


def share_of(planes, tokens):
    share = 1
    while share * 2 <= SHARE and planes % (share * 2) == 0 and tokens % (share * 32) == 0:
        share *= 2
    return share


def reduce_kernel(
    ndp, nmp, share,
    act, og, weight, row_moment, col_moment,
    grad, held_weight, new_rows, new_cols, coefs,
    feat, feat_t, gbuf, row_acc, col_acc, row_slots, col_slots, row_scale, col_scale,
    sum_mp, sum_dp,
    local_sem, weight_sem,
    a_send, a_recv, ab_send, ab_recv, az_send, az_recv,
    ix_send, ix_recv, iy_send, iy_recv,
    jx_send, jx_recv, jy_send, jy_recv,
    o_send, o_recv, bx_send, bx_recv, by_send, by_recv,
    cx_send, cx_recv, cy_send, cy_recv,
    r_send, r_recv, c_send, c_recv, p_send, p_recv, q_send, q_recv,
):
    me = lax.axis_index("dp")
    plane = lax.axis_index("mp")
    chips = ndp // 2
    ny, nx = grid_of(chips)
    core = lax.rem(me, 2)
    chip = me // 2
    x = lax.rem(chip, nx)
    y = chip // nx
    sibling = me + 1 - 2 * core
    rows, cols = grad.shape
    tokens = ndp * gbuf.shape[2] * gbuf.shape[3]
    width = cols // BLOCKS
    part = lax.rem(plane, share)
    base = plane - part

    def index_of(yy, xx, cc):
        return (yy * nx + xx) * 2 + cc

    def x_at(k):
        return lax.rem(x + k + nx, nx)

    def y_at(k):
        return lax.rem(y + k + ny, ny)

    def at_dp(d):
        return {"dp": d, "mp": plane}

    def at_mp(z):
        return {"dp": me, "mp": z}

    sends = []

    def send(src, dst, send_sem, recv_sem, device):
        copy = pltpu.make_async_remote_copy(
            src_ref=src, dst_ref=dst, send_sem=send_sem, recv_sem=recv_sem,
            device_id=device, device_id_type=MESH,
        )
        copy.start()
        sends.append(copy)

    def arrived(ref, recv_sem, send_sem):
        pltpu.make_async_remote_copy(
            src_ref=ref, dst_ref=ref, send_sem=send_sem, recv_sem=recv_sem,
            device_id=at_dp(sibling), device_id_type=MESH,
        ).wait_recv()

    def feature_cols(d):
        return pl.ds(pl.multiple_of(d * rows, rows), rows)

    weight_rows = rows // 4
    weight_copies = [
        pltpu.make_async_copy(
            weight.at[pl.ds(i * weight_rows, weight_rows)],
            held_weight.at[pl.ds(i * weight_rows, weight_rows)],
            weight_sem.at[i],
        )
        for i in range(4)
    ]
    own_features = pltpu.make_async_copy(act.at[:, :, feature_cols(me)], feat.at[me], local_sem.at[BLOCKS])
    own_features.start()
    own_blocks = []
    for b in range(BLOCKS):
        own_blocks.append(
            pltpu.make_async_copy(og.at[:, :, pl.ds(b * width, width)], gbuf.at[b, me], local_sem.at[b])
        )
        own_blocks[b].start()

    barrier = pltpu.get_barrier_semaphore()
    for k in range(1, ndp):
        pl.semaphore_signal(barrier, inc=1, device_id=at_dp(lax.rem(me + k, ndp)), device_id_type=MESH)
    for k in range(1, nmp):
        pl.semaphore_signal(barrier, inc=1, device_id=at_mp(lax.rem(plane + k, nmp)), device_id_type=MESH)
    pl.semaphore_wait(barrier, ndp + nmp - 2)

    for k in range(1, chips):
        other = lax.rem(chip + k, chips)
        for c in range(2):
            there = 2 * other + c
            send(act.at[part, :, feature_cols(there)], feat.at[me, part], a_send.at[k, c], a_recv.at[k, core], at_dp(there))

    def half(h, b):
        return og.at[h, :, pl.ds(b * width, width)]

    def first_hops(b):
        for k in range(1, nx):
            send(half(0, b), gbuf.at[b, me, 0], ix_send.at[b, k], ix_recv.at[b, k], at_dp(index_of(y, x_at(k), core)))
        for k in range(1, ny):
            send(half(1, b), gbuf.at[b, me, 1], iy_send.at[b, k], iy_recv.at[b, k], at_dp(index_of(y_at(k), x, core)))

    first_hops(0)
    send(act.at[:, :, feature_cols(sibling)], feat.at[me], ab_send.at[0], ab_recv.at[0], at_dp(sibling))
    for copy in weight_copies:
        copy.start()
    first_hops(1)
    for b in range(BLOCKS):
        send(og.at[:, :, pl.ds(b * width, width)], gbuf.at[b, me], o_send.at[b], o_recv.at[b], at_dp(sibling))

    for k in range(1, chips):
        source = lax.rem(chip + chips - k, chips)
        for c in range(2):
            arrived(feat.at[2 * source + c, part], a_recv.at[k, c], a_send.at[k, c])
        for j in range(1, share):
            block = feat.at[pl.ds(2 * source, 2), part]
            send(block, block, az_send.at[k, j], az_recv.at[k, j], at_mp(base + lax.rem(part + j, share)))

    def second_hops(b):
        for j in range(nx):
            source = index_of(y, x_at(-j), core)
            block = gbuf.at[b, source, 0]
            if j:
                arrived(block, ix_recv.at[b, j], ix_send.at[b, j])
            for k in range(1, ny):
                send(half(0, b) if j == 0 else block, block, jy_send.at[b, j, k], jy_recv.at[b, j, k], at_dp(index_of(y_at(k), x, core)))
        for j in range(ny):
            source = index_of(y_at(-j), x, core)
            block = gbuf.at[b, source, 1]
            if j:
                arrived(block, iy_recv.at[b, j], iy_send.at[b, j])
            for k in range(1, nx):
                send(half(1, b) if j == 0 else block, block, jx_send.at[b, j, k], jx_recv.at[b, j, k], at_dp(index_of(y, x_at(k), core)))
        for j in range(1, nx):
            block = gbuf.at[b, index_of(y, x_at(-j), core), 0]
            send(block, block, bx_send.at[b, j], bx_recv.at[b, j], at_dp(sibling))
        for j in range(1, ny):
            block = gbuf.at[b, index_of(y_at(-j), x, core), 1]
            send(block, block, by_send.at[b, j], by_recv.at[b, j], at_dp(sibling))

    def to_sibling(b):
        for k in range(1, ny):
            for j in range(nx):
                block = gbuf.at[b, index_of(y_at(-k), x_at(-j), core), 0]
                arrived(block, jy_recv.at[b, j, k], jy_send.at[b, j, k])
                send(block, block, cy_send.at[b, j, k], cy_recv.at[b, j, k], at_dp(sibling))
        for k in range(1, nx):
            for j in range(ny):
                block = gbuf.at[b, index_of(y_at(-j), x_at(-k), core), 1]
                arrived(block, jx_recv.at[b, j, k], jx_send.at[b, j, k])
                send(block, block, cx_send.at[b, j, k], cx_recv.at[b, j, k], at_dp(sibling))

    def block_ready(b):
        other = 1 - core
        own_blocks[b].wait()
        arrived(gbuf.at[b, sibling], o_recv.at[b], o_send.at[b])
        for j in range(1, nx):
            arrived(gbuf.at[b, index_of(y, x_at(-j), other), 0], bx_recv.at[b, j], bx_send.at[b, j])
        for j in range(1, ny):
            arrived(gbuf.at[b, index_of(y_at(-j), x, other), 1], by_recv.at[b, j], by_send.at[b, j])
        for k in range(1, ny):
            for j in range(nx):
                arrived(gbuf.at[b, index_of(y_at(-k), x_at(-j), other), 0], cy_recv.at[b, j, k], cy_send.at[b, j, k])
        for k in range(1, nx):
            for j in range(ny):
                arrived(gbuf.at[b, index_of(y_at(-j), x_at(-k), other), 1], cx_recv.at[b, j, k], cx_send.at[b, j, k])

    def features_ready():
        own_features.wait()
        arrived(feat.at[sibling], ab_recv.at[0], ab_send.at[0])
        for k in range(1, chips):
            source = lax.rem(chip + chips - k, chips)
            for j in range(1, share):
                block = feat.at[pl.ds(2 * source, 2), lax.rem(part - j + share, share)]
                arrived(block, az_recv.at[k, j], az_send.at[k, j])
        shard = tokens // ndp
        for d in range(ndp):
            feat_t[:, d * shard:(d + 1) * shard] = feat[d].reshape(shard, rows).T

    tile = min(rows, 256)
    narrow = min(width, 512)

    def multiply(b):
        def body(i, carry):
            here = pl.ds(pl.multiple_of(i * tile, tile), tile)
            left = feat_t[here, :]
            for n in range(width // narrow):
                right = gbuf[b, :, :, :, n * narrow:(n + 1) * narrow].reshape(tokens, narrow)
                product = jnp.dot(left, right, preferred_element_type=F32)
                at = b * width + n * narrow
                grad[here, at:at + narrow] = product
                squares = product * product
                total = squares[:, :LANES]
                for l in range(1, narrow // LANES):
                    total = total + squares[:, l * LANES:(l + 1) * LANES]
                row_acc[here, :] += total
                col_acc[:, at:at + narrow] += jnp.sum(squares, axis=0, keepdims=True)
            return carry

        lax.fori_loop(0, rows // tile, body, 0)

    step = 32

    def weight_norm():
        for copy in weight_copies:
            copy.wait()

        def body(i, total):
            here = pl.ds(pl.multiple_of(i * step, step), step)
            for l in range(cols // LANES):
                piece = held_weight[here, l * LANES:(l + 1) * LANES]
                total = total + piece * piece
            return total

        return lax.fori_loop(0, rows // step, body, jnp.zeros((step, LANES), F32))

    row_acc[...] = jnp.zeros_like(row_acc)
    col_acc[...] = jnp.zeros_like(col_acc)

    second_hops(0)
    first_hops(2)
    weight_squares = weight_norm()
    second_hops(1)
    first_hops(3)
    to_sibling(0)
    second_hops(2)
    to_sibling(1)
    features_ready()
    block_ready(0)
    multiply(0)
    second_hops(3)
    to_sibling(2)
    block_ready(1)
    multiply(1)
    to_sibling(3)
    block_ready(2)
    multiply(2)
    block_ready(3)
    multiply(3)

    col_slots[me] = col_acc[...]
    for k in range(1, ndp):
        send(col_slots.at[me], col_slots.at[me], c_send.at[k], c_recv.at[k], at_dp(lax.rem(me + k, ndp)))
    row_slots[plane] = jnp.sum(row_acc[...].T, axis=0, keepdims=True)
    for k in range(1, nmp):
        send(row_slots.at[plane], row_slots.at[plane], r_send.at[k], r_recv.at[k], at_mp(lax.rem(plane + k, nmp)))
    for k in range(1, nmp):
        arrived(row_slots.at[lax.rem(plane + nmp - k, nmp)], r_recv.at[k], r_send.at[k])
    row_total = row_slots[0]
    for k in range(1, nmp):
        row_total = row_total + row_slots[k]
    rows_now = BETA_TWO * row_moment[...] + (1.0 - BETA_TWO) * (row_total / FF)
    new_rows[...] = rows_now
    row_scale[...] = jnp.broadcast_to(1.0 / jnp.sqrt(rows_now), (LANES, rows)).T
    for k in range(1, ndp):
        arrived(col_slots.at[lax.rem(me + ndp - k, ndp)], c_recv.at[k], c_send.at[k])
    col_total = col_slots[0]
    for k in range(1, ndp):
        col_total = col_total + col_slots[k]
    cols_now = BETA_TWO * col_moment[...] + (1.0 - BETA_TWO) * (col_total / D)
    new_cols[...] = cols_now
    col_scale[...] = 1.0 / jnp.sqrt(cols_now)

    def scale(i, totals):
        ss, sw = totals
        here = pl.ds(pl.multiple_of(i * step, step), step)
        by_row = row_scale[here, :]
        for l in range(cols // LANES):
            at = slice(l * LANES, (l + 1) * LANES)
            value = grad[here, at] * col_scale[:, at] * by_row
            grad[here, at] = value
            ss = ss + value * value
            sw = sw + value * held_weight[here, at]
        return ss, sw

    zero = jnp.zeros((step, LANES), F32)
    ss, sw = lax.fori_loop(0, rows // step, scale, (zero, zero))
    for i, total in enumerate((ss, sw, weight_squares)):
        sum_mp[plane, :, i * LANES:(i + 1) * LANES] = jnp.sum(total, axis=0, keepdims=True)
    for k in range(1, nmp):
        send(sum_mp.at[plane], sum_mp.at[plane], p_send.at[k], p_recv.at[k], at_mp(lax.rem(plane + k, nmp)))
    for k in range(1, nmp):
        arrived(sum_mp.at[lax.rem(plane + nmp - k, nmp)], p_recv.at[k], p_send.at[k])
    total = sum_mp[0]
    for k in range(1, nmp):
        total = total + sum_mp[k]
    sum_dp[me] = total
    for k in range(1, ndp):
        send(sum_dp.at[me], sum_dp.at[me], q_send.at[k], q_recv.at[k], at_dp(lax.rem(me + k, ndp)))
    for k in range(1, ndp):
        arrived(sum_dp.at[lax.rem(me + ndp - k, ndp)], q_recv.at[k], q_send.at[k])
    total = sum_dp[0]
    for k in range(1, ndp):
        total = total + sum_dp[k]
    scaled_sum, cross_sum, weight_sum = (
        jnp.broadcast_to(jnp.sum(total[:, i * LANES:(i + 1) * LANES], axis=1, keepdims=True), (1, LANES))
        for i in range(3)
    )
    factor = 1.0 / jnp.maximum(1.0, jnp.sqrt(scaled_sum / (D * FF)) / CLIP_LEVEL)
    direction_sum = (
        factor * factor * scaled_sum
        + (2.0 * WEIGHT_DECAY) * factor * cross_sum
        + (WEIGHT_DECAY * WEIGHT_DECAY) * weight_sum
    )
    trust_ratio = jnp.sqrt(weight_sum / (jnp.maximum(direction_sum, 0.0) + EPSILON))
    coefs[0:1, :] = trust_ratio * factor
    coefs[1:2, :] = trust_ratio * WEIGHT_DECAY
    for copy in sends:
        copy.wait_send()


def update_kernel(scaled, weight, coefs, out):
    rows, cols = out.shape
    here = pl.ds(pl.multiple_of(pl.program_id(0) * rows, rows), rows)
    by_scaled = coefs[0:1, :]
    by_weight = coefs[1:2, :]
    for l in range(cols // LANES):
        at = slice(l * LANES, (l + 1) * LANES)
        out[:, at] = by_scaled * scaled[here, at] + by_weight * weight[here, at]


def shards(ndp, nmp, activations, out_grads, weight, row_moment, col_moment):
    shard = activations.shape[0]
    rows, cols = weight.shape
    tokens = ndp * shard
    width = cols // BLOCKS
    chips = ndp // 2
    ny, nx = grid_of(chips)
    share = share_of(nmp, shard)
    part = shard // share
    vmem = pl.BlockSpec(memory_space=pltpu.VMEM)
    hbm = pl.BlockSpec(memory_space=pl.ANY)
    dma = pltpu.SemaphoreType.DMA

    def pair(*shape):
        return [dma(shape), dma(shape)]

    grad, held_weight, new_rows, new_cols, coefs = pl.pallas_call(
        functools.partial(reduce_kernel, ndp, nmp, share),
        out_shape=[
            pltpu.VMEM((rows, cols), F32),
            pltpu.VMEM((rows, cols), F32),
            jax.ShapeDtypeStruct((1, rows), F32),
            jax.ShapeDtypeStruct((1, cols), F32),
            pltpu.VMEM((2, LANES), F32),
        ],
        in_specs=[hbm, hbm, hbm, vmem, vmem],
        out_specs=[vmem] * 5,
        scratch_shapes=[
            pltpu.VMEM((ndp, share, part, rows), jnp.bfloat16),
            pltpu.VMEM((rows, tokens), jnp.bfloat16),
            pltpu.VMEM((BLOCKS, ndp, 2, shard // 2, width), jnp.bfloat16),
            pltpu.VMEM((rows, LANES), F32),
            pltpu.VMEM((1, cols), F32),
            pltpu.VMEM((nmp, 1, rows), F32),
            pltpu.VMEM((ndp, 1, cols), F32),
            pltpu.VMEM((rows, LANES), F32),
            pltpu.VMEM((1, cols), F32),
            pltpu.VMEM((nmp, 1, 3 * LANES), F32),
            pltpu.VMEM((ndp, 1, 3 * LANES), F32),
            dma((BLOCKS + 1,)),
            dma((4,)),
            *pair(chips, 2), *pair(1), *pair(chips, share),
            *pair(BLOCKS, nx), *pair(BLOCKS, ny),
            *pair(BLOCKS, ny, nx), *pair(BLOCKS, nx, ny),
            *pair(BLOCKS), *pair(BLOCKS, nx), *pair(BLOCKS, ny),
            *pair(BLOCKS, ny, nx), *pair(BLOCKS, nx, ny),
            *pair(nmp), *pair(ndp), *pair(nmp), *pair(ndp),
        ],
        compiler_params=pltpu.CompilerParams(
            collective_id=0, has_side_effects=True, vmem_limit_bytes=22 * 2**20
        ),
        cost_estimate=pl.CostEstimate(
            flops=2 * rows * cols * tokens, bytes_accessed=8 * rows * cols, transcendentals=0
        ),
        name="gradient",
    )(
        activations.reshape(share, part, ndp * rows),
        out_grads.reshape(2, shard // 2, cols),
        weight,
        row_moment.reshape(1, rows),
        col_moment.reshape(1, cols),
    )
    tile = min(rows, 128)
    update = pl.pallas_call(
        update_kernel,
        out_shape=jax.ShapeDtypeStruct((rows, cols), F32),
        grid=(rows // tile,),
        in_specs=[vmem, vmem, vmem],
        out_specs=pl.BlockSpec((tile, cols), lambda i: (i, 0)),
        compiler_params=pltpu.CompilerParams(vmem_limit_bytes=12 * 2**20),
        cost_estimate=pl.CostEstimate(flops=3 * rows * cols, bytes_accessed=4 * rows * cols, transcendentals=0),
        name="update",
    )(
        pltpu.with_memory_space_constraint(grad, pltpu.VMEM),
        pltpu.with_memory_space_constraint(held_weight, pltpu.VMEM),
        pltpu.with_memory_space_constraint(coefs, pltpu.VMEM),
    )
    return update, new_rows.reshape(rows), new_cols.reshape(cols)


def solution(mesh):
    placed = (P("dp", None), P("dp", "mp"), P("dp", "mp"), P("dp"), P("mp"))
    return jax.shard_map(
        functools.partial(shards, mesh.shape["dp"], mesh.shape["mp"]),
        mesh=mesh,
        in_specs=placed,
        out_specs=(P("dp", "mp"), P("dp"), P("mp")),
        check_vma=False,
    )
```

```python
import functools
import math

import jax
import jax.numpy as jnp
from jax import lax
from jax.experimental import pallas as pl
from jax.experimental.pallas import tpu as pltpu
from jax.sharding import PartitionSpec as P

D = 8192
FF = 16384

BETA_TWO = 0.8
CLIP_LEVEL = 0.25
WEIGHT_DECAY = 0.1
EPSILON = 1e-06

MESH = pl.DeviceIdType.MESH
F32 = jnp.float32
BLOCKS = 8
READY = 5
GRANT = 22 * 2**20
SHARE = 2
LANES = 128


def grid_of(chips):
    wide = max(k for k in range(1, math.isqrt(chips) + 1) if chips % k == 0)
    return chips // wide, wide


def share_of(planes, tokens):
    share = 1
    while share * 2 <= SHARE and planes % (share * 2) == 0 and tokens % (share * 32) == 0:
        share *= 2
    return share


def reduce_kernel(
    ndp, nmp, share,
    act, og, weight, row_moment, col_moment,
    grad, held_weight, row_scale, new_rows, new_cols, coefs,
    feat, feat_t, gbuf, row_acc, ss_acc, sw_acc, row_slots, col_slots, sum_mp, sum_dp,
    local_sem, weight_sem,
    a_send, a_recv, ab_send, ab_recv, az_send, az_recv,
    ix_send, ix_recv, iy_send, iy_recv,
    jx_send, jx_recv, jy_send, jy_recv,
    o_send, o_recv, bx_send, bx_recv, by_send, by_recv,
    cx_send, cx_recv, cy_send, cy_recv,
    r_send, r_recv, c_send, c_recv, p_send, p_recv, q_send, q_recv,
):
    me = lax.axis_index("dp")
    plane = lax.axis_index("mp")
    chips = ndp // 2
    ny, nx = grid_of(chips)
    core = lax.rem(me, 2)
    chip = me // 2
    x = lax.rem(chip, nx)
    y = chip // nx
    sibling = me + 1 - 2 * core
    rows, cols = grad.shape
    tokens = ndp * gbuf.shape[2] * gbuf.shape[3]
    width = cols // BLOCKS
    part = lax.rem(plane, share)
    base = plane - part

    def index_of(yy, xx, cc):
        return (yy * nx + xx) * 2 + cc

    def x_at(k):
        return lax.rem(x + k + nx, nx)

    def y_at(k):
        return lax.rem(y + k + ny, ny)

    def at_dp(d):
        return {"dp": d, "mp": plane}

    def at_mp(z):
        return {"dp": me, "mp": z}

    sends = []

    def send(src, dst, send_sem, recv_sem, device):
        copy = pltpu.make_async_remote_copy(
            src_ref=src, dst_ref=dst, send_sem=send_sem, recv_sem=recv_sem,
            device_id=device, device_id_type=MESH,
        )
        copy.start()
        sends.append(copy)

    def arrived(ref, recv_sem, send_sem):
        pltpu.make_async_remote_copy(
            src_ref=ref, dst_ref=ref, send_sem=send_sem, recv_sem=recv_sem,
            device_id=at_dp(sibling), device_id_type=MESH,
        ).wait_recv()

    def feature_cols(d):
        return pl.ds(pl.multiple_of(d * rows, rows), rows)

    weight_rows = rows // 4
    weight_copies = [
        pltpu.make_async_copy(
            weight.at[pl.ds(i * weight_rows, weight_rows)],
            held_weight.at[pl.ds(i * weight_rows, weight_rows)],
            weight_sem.at[i],
        )
        for i in range(4)
    ]
    own_features = pltpu.make_async_copy(act.at[:, :, feature_cols(me)], feat.at[me], local_sem.at[BLOCKS])
    own_features.start()
    own_blocks = []
    for b in range(BLOCKS):
        own_blocks.append(
            pltpu.make_async_copy(og.at[:, :, pl.ds(b * width, width)], gbuf.at[b, me], local_sem.at[b])
        )
        own_blocks[b].start()

    barrier = pltpu.get_barrier_semaphore()
    for k in range(1, ndp):
        pl.semaphore_signal(barrier, inc=1, device_id=at_dp(lax.rem(me + k, ndp)), device_id_type=MESH)
    for k in range(1, nmp):
        pl.semaphore_signal(barrier, inc=1, device_id=at_mp(lax.rem(plane + k, nmp)), device_id_type=MESH)
    pl.semaphore_wait(barrier, ndp + nmp - 2)

    for k in range(1, chips):
        other = lax.rem(chip + k, chips)
        for c in range(2):
            there = 2 * other + c
            send(act.at[part, :, feature_cols(there)], feat.at[me, part], a_send.at[k, c], a_recv.at[k, core], at_dp(there))

    def half(h, b):
        return og.at[h, :, pl.ds(b * width, width)]

    def first_hops(b):
        for k in range(1, nx):
            send(half(0, b), gbuf.at[b, me, 0], ix_send.at[b, k], ix_recv.at[b, k], at_dp(index_of(y, x_at(k), core)))
        for k in range(1, ny):
            send(half(1, b), gbuf.at[b, me, 1], iy_send.at[b, k], iy_recv.at[b, k], at_dp(index_of(y_at(k), x, core)))

    first_hops(0)
    send(act.at[:, :, feature_cols(sibling)], feat.at[me], ab_send.at[0], ab_recv.at[0], at_dp(sibling))
    for copy in weight_copies:
        copy.start()
    first_hops(1)
    for b in range(BLOCKS):
        send(og.at[:, :, pl.ds(b * width, width)], gbuf.at[b, me], o_send.at[b], o_recv.at[b], at_dp(sibling))

    for k in range(1, chips):
        source = lax.rem(chip + chips - k, chips)
        for c in range(2):
            arrived(feat.at[2 * source + c, part], a_recv.at[k, c], a_send.at[k, c])
        for j in range(1, share):
            block = feat.at[pl.ds(2 * source, 2), part]
            send(block, block, az_send.at[k, j], az_recv.at[k, j], at_mp(base + lax.rem(part + j, share)))

    def second_hops(b):
        for j in range(nx):
            source = index_of(y, x_at(-j), core)
            block = gbuf.at[b, source, 0]
            if j:
                arrived(block, ix_recv.at[b, j], ix_send.at[b, j])
            for k in range(1, ny):
                send(half(0, b) if j == 0 else block, block, jy_send.at[b, j, k], jy_recv.at[b, j, k], at_dp(index_of(y_at(k), x, core)))
        for j in range(ny):
            source = index_of(y_at(-j), x, core)
            block = gbuf.at[b, source, 1]
            if j:
                arrived(block, iy_recv.at[b, j], iy_send.at[b, j])
            for k in range(1, nx):
                send(half(1, b) if j == 0 else block, block, jx_send.at[b, j, k], jx_recv.at[b, j, k], at_dp(index_of(y, x_at(k), core)))
        for j in range(1, nx):
            block = gbuf.at[b, index_of(y, x_at(-j), core), 0]
            send(block, block, bx_send.at[b, j], bx_recv.at[b, j], at_dp(sibling))
        for j in range(1, ny):
            block = gbuf.at[b, index_of(y_at(-j), x, core), 1]
            send(block, block, by_send.at[b, j], by_recv.at[b, j], at_dp(sibling))

    def to_sibling(b):
        for k in range(1, ny):
            for j in range(nx):
                block = gbuf.at[b, index_of(y_at(-k), x_at(-j), core), 0]
                arrived(block, jy_recv.at[b, j, k], jy_send.at[b, j, k])
                send(block, block, cy_send.at[b, j, k], cy_recv.at[b, j, k], at_dp(sibling))
        for k in range(1, nx):
            for j in range(ny):
                block = gbuf.at[b, index_of(y_at(-j), x_at(-k), core), 1]
                arrived(block, jx_recv.at[b, j, k], jx_send.at[b, j, k])
                send(block, block, cx_send.at[b, j, k], cx_recv.at[b, j, k], at_dp(sibling))

    def block_ready(b):
        other = 1 - core
        own_blocks[b].wait()
        arrived(gbuf.at[b, sibling], o_recv.at[b], o_send.at[b])
        for j in range(1, nx):
            arrived(gbuf.at[b, index_of(y, x_at(-j), other), 0], bx_recv.at[b, j], bx_send.at[b, j])
        for j in range(1, ny):
            arrived(gbuf.at[b, index_of(y_at(-j), x, other), 1], by_recv.at[b, j], by_send.at[b, j])
        for k in range(1, ny):
            for j in range(nx):
                arrived(gbuf.at[b, index_of(y_at(-k), x_at(-j), other), 0], cy_recv.at[b, j, k], cy_send.at[b, j, k])
        for k in range(1, nx):
            for j in range(ny):
                arrived(gbuf.at[b, index_of(y_at(-j), x_at(-k), other), 1], cx_recv.at[b, j, k], cx_send.at[b, j, k])

    def features_ready():
        own_features.wait()
        arrived(feat.at[sibling], ab_recv.at[0], ab_send.at[0])
        for k in range(1, chips):
            source = lax.rem(chip + chips - k, chips)
            for j in range(1, share):
                block = feat.at[pl.ds(2 * source, 2), lax.rem(part - j + share, share)]
                arrived(block, az_recv.at[k, j], az_send.at[k, j])
        shard = tokens // ndp
        for d in range(ndp):
            feat_t[:, d * shard:(d + 1) * shard] = feat[d].reshape(shard, rows).T

    tile = min(rows, 256)
    narrow = min(width, 512)

    def multiply(b):
        block_ready(b)

        def body(i, total):
            here = pl.ds(pl.multiple_of(i * tile, tile), tile)
            left = feat_t[here, :]
            parts = []
            for n in range(width // narrow):
                right = gbuf[b, :, :, :, n * narrow:(n + 1) * narrow].reshape(tokens, narrow)
                product = jnp.dot(left, right, preferred_element_type=F32)
                at = b * width + n * narrow
                grad[here, at:at + narrow] = product
                squares = product * product
                across = squares[:, :LANES]
                for l in range(1, narrow // LANES):
                    across = across + squares[:, l * LANES:(l + 1) * LANES]
                row_acc[here, :] += across
                parts.append(jnp.sum(squares, axis=0, keepdims=True))
            return total + (parts[0] if len(parts) == 1 else jnp.concatenate(parts, axis=1))

        col_slots[b, me] = lax.fori_loop(0, rows // tile, body, jnp.zeros((1, width), F32))
        for k in range(1, ndp):
            send(col_slots.at[b, me], col_slots.at[b, me], c_send.at[b, k], c_recv.at[b, k], at_dp(lax.rem(me + k, ndp)))

    def scale(b):
        for k in range(1, ndp):
            arrived(col_slots.at[b, lax.rem(me + ndp - k, ndp)], c_recv.at[b, k], c_send.at[b, k])
        col_total = col_slots[b, 0]
        for k in range(1, ndp):
            col_total = col_total + col_slots[b, k]
        block = slice(b * width, (b + 1) * width)
        cols_now = BETA_TWO * col_moment[:, block] + (1.0 - BETA_TWO) * (col_total / D)
        new_cols[:, block] = cols_now
        by_col = 1.0 / jnp.sqrt(cols_now)

        def body(i, carry):
            here = pl.ds(pl.multiple_of(i * step, step), step)
            ss = ss_acc[here, :]
            sw = sw_acc[here, :]
            for l in range(width // LANES):
                at = slice(b * width + l * LANES, b * width + (l + 1) * LANES)
                value = grad[here, at] * by_col[:, l * LANES:(l + 1) * LANES]
                grad[here, at] = value
                ss = ss + value * value
                sw = sw + value * held_weight[here, at]
            ss_acc[here, :] = ss
            sw_acc[here, :] = sw
            return carry

        lax.fori_loop(0, rows // step, body, 0)

    step = 32

    def weight_norm():
        for copy in weight_copies:
            copy.wait()

        def body(i, total):
            here = pl.ds(pl.multiple_of(i * step, step), step)
            for l in range(cols // LANES):
                piece = held_weight[here, l * LANES:(l + 1) * LANES]
                total = total + piece * piece
            return total

        return lax.fori_loop(0, rows // step, body, jnp.zeros((step, LANES), F32))

    for acc in (row_acc, ss_acc, sw_acc):
        acc[...] = jnp.zeros_like(acc)
    multiplied = scaled = 0
    for b in range(BLOCKS):
        second_hops(b)
        if b + 2 < BLOCKS:
            first_hops(b + 2)
        if b == 0:
            weight_squares = weight_norm()
        else:
            to_sibling(b - 1)
        if b == READY:
            features_ready()
        if b >= READY:
            for _ in range(2):
                multiply(multiplied)
                multiplied += 1
            while scaled < multiplied - 2:
                scale(scaled)
                scaled += 1
    while multiplied < BLOCKS - 1:
        multiply(multiplied)
        multiplied += 1
    to_sibling(BLOCKS - 1)
    multiply(BLOCKS - 1)

    row_slots[plane] = jnp.sum(row_acc[...].T, axis=0, keepdims=True)
    for k in range(1, nmp):
        send(row_slots.at[plane], row_slots.at[plane], r_send.at[k], r_recv.at[k], at_mp(lax.rem(plane + k, nmp)))
    while scaled < BLOCKS - 1:
        scale(scaled)
        scaled += 1
    for k in range(1, nmp):
        arrived(row_slots.at[lax.rem(plane + nmp - k, nmp)], r_recv.at[k], r_send.at[k])
    row_total = row_slots[0]
    for k in range(1, nmp):
        row_total = row_total + row_slots[k]
    rows_now = BETA_TWO * row_moment[...] + (1.0 - BETA_TWO) * (row_total / FF)
    new_rows[...] = rows_now
    row_scale[...] = jnp.broadcast_to(1.0 / jnp.sqrt(rows_now), (LANES, rows)).T
    scale(BLOCKS - 1)

    def weigh(i, totals):
        ss, sw = totals
        here = pl.ds(pl.multiple_of(i * step, step), step)
        by_row = row_scale[here, :]
        return ss + ss_acc[here, :] * (by_row * by_row), sw + sw_acc[here, :] * by_row

    zero = jnp.zeros((step, LANES), F32)
    ss, sw = lax.fori_loop(0, rows // step, weigh, (zero, zero))
    for i, total in enumerate((ss, sw, weight_squares)):
        sum_mp[plane, :, i * LANES:(i + 1) * LANES] = jnp.sum(total, axis=0, keepdims=True)
    for k in range(1, nmp):
        send(sum_mp.at[plane], sum_mp.at[plane], p_send.at[k], p_recv.at[k], at_mp(lax.rem(plane + k, nmp)))
    for k in range(1, nmp):
        arrived(sum_mp.at[lax.rem(plane + nmp - k, nmp)], p_recv.at[k], p_send.at[k])
    total = sum_mp[0]
    for k in range(1, nmp):
        total = total + sum_mp[k]
    sum_dp[me] = total
    for k in range(1, ndp):
        send(sum_dp.at[me], sum_dp.at[me], q_send.at[k], q_recv.at[k], at_dp(lax.rem(me + k, ndp)))
    for k in range(1, ndp):
        arrived(sum_dp.at[lax.rem(me + ndp - k, ndp)], q_recv.at[k], q_send.at[k])
    total = sum_dp[0]
    for k in range(1, ndp):
        total = total + sum_dp[k]
    scaled_sum, cross_sum, weight_sum = (
        jnp.broadcast_to(jnp.sum(total[:, i * LANES:(i + 1) * LANES], axis=1, keepdims=True), (1, LANES))
        for i in range(3)
    )
    factor = 1.0 / jnp.maximum(1.0, jnp.sqrt(scaled_sum / (D * FF)) / CLIP_LEVEL)
    direction_sum = (
        factor * factor * scaled_sum
        + (2.0 * WEIGHT_DECAY) * factor * cross_sum
        + (WEIGHT_DECAY * WEIGHT_DECAY) * weight_sum
    )
    trust_ratio = jnp.sqrt(weight_sum / (jnp.maximum(direction_sum, 0.0) + EPSILON))
    coefs[0:1, :] = trust_ratio * factor
    coefs[1:2, :] = trust_ratio * WEIGHT_DECAY
    for copy in sends:
        copy.wait_send()


def update_kernel(scaled, weight, row_scale, coefs, rows_in, cols_in, out, rows_out, cols_out):
    rows, cols = out.shape
    here = pl.ds(pl.multiple_of(pl.program_id(0) * rows, rows), rows)
    by_row = row_scale[here, :] * coefs[0:1, :]
    by_weight = coefs[1:2, :]
    for l in range(cols // LANES):
        at = slice(l * LANES, (l + 1) * LANES)
        out[:, at] = by_row * scaled[here, at] + by_weight * weight[here, at]

    @pl.when(pl.program_id(0) == 0)
    def _():
        rows_out[...] = rows_in[...]
        cols_out[...] = cols_in[...]


def shards(ndp, nmp, activations, out_grads, weight, row_moment, col_moment):
    shard = activations.shape[0]
    rows, cols = weight.shape
    tokens = ndp * shard
    width = cols // BLOCKS
    chips = ndp // 2
    ny, nx = grid_of(chips)
    share = share_of(nmp, shard)
    part = shard // share
    vmem = pl.BlockSpec(memory_space=pltpu.VMEM)
    hbm = pl.BlockSpec(memory_space=pl.ANY)
    dma = pltpu.SemaphoreType.DMA

    def pair(*shape):
        return [dma(shape), dma(shape)]

    held = pl.pallas_call(
        functools.partial(reduce_kernel, ndp, nmp, share),
        out_shape=[
            pltpu.VMEM((rows, cols), F32),
            pltpu.VMEM((rows, cols), F32),
            pltpu.VMEM((rows, LANES), F32),
            pltpu.VMEM((1, rows), F32),
            pltpu.VMEM((1, cols), F32),
            pltpu.VMEM((2, LANES), F32),
        ],
        in_specs=[hbm, hbm, hbm, vmem, vmem],
        out_specs=[vmem] * 6,
        scratch_shapes=[
            pltpu.VMEM((ndp, share, part, rows), jnp.bfloat16),
            pltpu.VMEM((rows, tokens), jnp.bfloat16),
            pltpu.VMEM((BLOCKS, ndp, 2, shard // 2, width), jnp.bfloat16),
            pltpu.VMEM((rows, LANES), F32),
            pltpu.VMEM((rows, LANES), F32),
            pltpu.VMEM((rows, LANES), F32),
            pltpu.VMEM((nmp, 1, rows), F32),
            pltpu.VMEM((BLOCKS, ndp, 1, width), F32),
            pltpu.VMEM((nmp, 1, 3 * LANES), F32),
            pltpu.VMEM((ndp, 1, 3 * LANES), F32),
            dma((BLOCKS + 1,)),
            dma((4,)),
            *pair(chips, 2), *pair(1), *pair(chips, share),
            *pair(BLOCKS, nx), *pair(BLOCKS, ny),
            *pair(BLOCKS, ny, nx), *pair(BLOCKS, nx, ny),
            *pair(BLOCKS), *pair(BLOCKS, nx), *pair(BLOCKS, ny),
            *pair(BLOCKS, ny, nx), *pair(BLOCKS, nx, ny),
            *pair(nmp), *pair(BLOCKS, ndp), *pair(nmp), *pair(ndp),
        ],
        compiler_params=pltpu.CompilerParams(
            collective_id=0, has_side_effects=True, vmem_limit_bytes=GRANT
        ),
        cost_estimate=pl.CostEstimate(
            flops=2 * rows * cols * tokens, bytes_accessed=8 * rows * cols, transcendentals=0
        ),
        name="gradient",
    )(
        activations.reshape(share, part, ndp * rows),
        out_grads.reshape(2, shard // 2, cols),
        weight,
        row_moment.reshape(1, rows),
        col_moment.reshape(1, cols),
    )
    tile = min(rows, 64)
    whole = lambda i: (0, 0)
    update, new_rows, new_cols = pl.pallas_call(
        update_kernel,
        out_shape=[
            jax.ShapeDtypeStruct((rows, cols), F32),
            jax.ShapeDtypeStruct((1, rows), F32),
            jax.ShapeDtypeStruct((1, cols), F32),
        ],
        grid=(rows // tile,),
        in_specs=[vmem, vmem, vmem, vmem, vmem, vmem],
        out_specs=[
            pl.BlockSpec((tile, cols), lambda i: (i, 0)),
            pl.BlockSpec((1, rows), whole),
            pl.BlockSpec((1, cols), whole),
        ],
        compiler_params=pltpu.CompilerParams(vmem_limit_bytes=GRANT),
        cost_estimate=pl.CostEstimate(flops=3 * rows * cols, bytes_accessed=4 * rows * cols, transcendentals=0),
        name="update",
    )(
        *(pltpu.with_memory_space_constraint(held[i], pltpu.VMEM) for i in (0, 1, 2, 5, 3, 4))
    )
    return update, new_rows.reshape(rows), new_cols.reshape(cols)


def solution(mesh):
    placed = (P("dp", None), P("dp", "mp"), P("dp", "mp"), P("dp"), P("mp"))
    return jax.shard_map(
        functools.partial(shards, mesh.shape["dp"], mesh.shape["mp"]),
        mesh=mesh,
        in_specs=placed,
        out_specs=(P("dp", "mp"), P("dp"), P("mp")),
        check_vma=False,
    )
```
